32 devices in a mesh: section: 2 (over core), expert: 8 (over z, y), dp: 2 (over x).
Axes of the slice: x: 2, y: 2, z: 4, core: 2. Of those that a mesh axis runs over, the one named last changes fastest.
Arguments:
- hidden_held: bfloat16 [2, 1024, 4096], P('section', 'expert'), may hold values from -6 to 6
- fresh_rows: bfloat16 [1, 1024, 4096], P(None, 'expert'), may hold values from -6 to 6
- doc_held: int32 [2, 1024], P('section', 'expert'), may hold values from 0 to 15, never falling along the last dimension, each value on 1 to 128 neighbouring positions
- doc_fresh: int32 [1, 1024], P(None, 'expert'), may hold values from 0 to 15, never falling along the last dimension, each value on 1 to 128 neighbouring positions
- routes: int32 [2, 2, 1024, 2], P(None, 'section', 'expert'), may hold values from 0 to 7, all different within a row; in each aligned block of 128 rows (0 to 127, 128 to 255, ..., all dimensions but the last counted through in order) at most 48 rows name the same one
- attn_gain: bfloat16 [2, 4096], P('section'), may hold values from 0.25 to 1.75
- query_gain: bfloat16 [2, 4096], P('section'), may hold values from -4 to 4
- key_gain: bfloat16 [2, 4096], P('section'), may hold values from -4 to 4
- ffn_gain: bfloat16 [2, 4096], P('section'), may hold values from 0.25 to 1.75
- router: bfloat16 [2, 4096, 8], P('section'), may hold values from -0.09375 to 0.09375
- weight_in: bfloat16 [2, 8, 4096, 2, 1536], P('section', 'expert', None, None, 'dp'), may hold values from -0.09375 to 0.09375
- weight_out: bfloat16 [2, 8, 1536, 4096], P('section', 'expert', 'dp'), may hold values from -0.15625 to 0.15625
Outputs:
- layer_out: bfloat16 [2, 2, 1024, 4096], P(None, 'section', 'expert')
The draws below stay inside these ranges and needn't reach their ends.
Inputs may be any that keep to these rules, and one draw needn't show every extreme that they name: `doc_held`: ids never fall along a row; every document has at most 128 tokens, and one has exactly 128. `doc_fresh`: ids never fall along a row; every document has at most 128 tokens, and one has exactly 128. `routes`: the 2 experts of a token differ; among the 128 tokens of one device for one step and layer, no expert is chosen more than 48 times, a bound that some block reaches.
All inputs are finite; a program needn't handle non-finite values.
Results may differ from the reference program's by a relative error of at most 0.017.
Values may be sent and summed in bfloat16 or wider, within the bound.
No kernel may reach another device: no remote copies, remote signals or barrier semaphores. Data moves between devices by JAX's collectives and lax.ppermute only.
A program may use at most 128 MiB of HBM per device.

```python
import math
import jax
import jax.numpy as jnp
import numpy as np
from jax import lax

D = 4096
HEAD_DIM = 128
EXPERT_HIDDEN = 1536
TOP = 2
TICKS = 2
TOK_DEV = 128
TOKENS = 1024
LAYERS = 2
EXPERTS = 8
CAP = 48
N_EXPERT = 8


def level_of(stream_key, shape, pieces, smallest, high):
    factor_of, own = 1.0, jax.random.fold_in(stream_key, 6)
    for axis_at, blocks in pieces:
        draws = jnp.exp(jax.random.uniform(jax.random.fold_in(own, axis_at), (blocks,), jnp.float32, smallest / len(pieces), high / len(pieces)))
        factor_of = factor_of * jnp.repeat(draws, shape[axis_at] // blocks).reshape([-1 if axis == axis_at else 1 for axis in range(len(shape))])
    return factor_of


def profile(count, total, limit, skew):
    weights = [(1 << 20) // math.isqrt(grade ** skew) + 1 for grade in range(2, count + 1)]
    rest, given = total - limit - (count - 1), [1] * (count - 1)
    while rest > 0:
        free = [i for i in range(count - 1) if given[i] < limit]
        pool, budget = sum([weights[i] for i in free]), rest
        for i in free:
            more = min(limit - given[i], max(1, budget * weights[i] // pool), rest)
            given[i] = given[i] + more
            rest = rest - more
    return np.array([limit] + given)


def uneven(own_key, amount, total, bound, slope):
    if amount == 2:
        one = jax.random.randint(own_key, (), max(1, total - bound), min(bound, total - 1) + 1)
        return jnp.stack([one, total - one])
    tallies = jnp.asarray(profile(amount, total, bound, slope), jnp.int32)
    couples = (amount - 1) // 2
    giver, sink = tallies[1:1 + 2 * couples:2], tallies[2:2 + 2 * couples:2]
    room = jnp.minimum(giver - 1, bound - sink)
    shifted = jax.random.randint(jax.random.fold_in(own_key, 1), (couples,), 0, 1 << 20) % (room + 1)
    tallies = tallies.at[1:1 + 2 * couples:2].set(giver - shifted).at[2:2 + 2 * couples:2].set(sink + shifted)
    return tallies[jax.random.permutation(jax.random.fold_in(own_key, 2), amount)]


def shared_out(rng, own, number, rows, number_of, top, limit, skew):
    sequence = jax.random.permutation(rng, number_of)
    heavy_load, ordinary = load_shares(number_of, rows * top, limit, skew, True), load_shares(number_of, rows * top, limit, skew, False)
    places = jnp.arange(number_of)

    def named(lengths, turn):
        used = int((lengths > 0).sum())
        fixed = max(1, used // 4)
        passed = fixed + (places - fixed + turn * (used - fixed)) % max(1, number_of - fixed)
        return jnp.zeros((number_of,), jnp.int32).at[sequence[jnp.where(places < fixed, places, passed)]].set(jnp.asarray(lengths, jnp.int32))

    lengths = jnp.where(number % 4 == 0, named(heavy_load, number // 4), named(ordinary, number - number // 4 - 1))
    mixed = jax.random.permutation(jax.random.fold_in(own, 3), number_of)
    donor, taker = mixed[0:number_of // 2 * 2:2], mixed[1:number_of // 2 * 2:2]
    room = jnp.minimum(lengths[donor] - 1, limit - lengths[taker]) // 2
    room = jnp.where((donor == sequence[0]) | (taker == sequence[0]) | (lengths[taker] == 0), 0, jnp.maximum(room, 0))
    passed = jax.random.randint(jax.random.fold_in(own, 4), (number_of // 2,), 0, 1 << 20) % (room + 1)
    lengths = lengths.at[donor].add(-passed).at[taker].add(passed)
    items = jnp.searchsorted(jnp.cumsum(lengths), jnp.arange(rows * top), side="right").astype(jnp.int32)
    table = items.reshape(top, rows).T
    table = table[jax.random.permutation(jax.random.fold_in(own, 1), rows)]
    turn = jax.random.randint(jax.random.fold_in(own, 2), (rows, 1), 0, top)
    return jnp.take_along_axis(table, (jnp.arange(top)[None, :] + turn) % top, axis=1)


def load_shares(amount, total, reach, skew, full):
    loads = [(1 << 20) // math.isqrt(standing ** skew) + 1 for standing in range(1, amount + 1)]
    largest = reach if full else min(reach, max(-(-total // amount), total * loads[0] // sum(loads)))
    least = 1 if total - largest >= amount - 1 else 0
    given, surplus = [largest] + [least] * (amount - 1), total - largest - least * (amount - 1)
    while surplus > 0:
        candidates = [i for i in range(1, amount) if given[i] < largest] or [i for i in range(1, amount) if given[i] < reach]
        mass, remaining = sum([loads[i] for i in candidates]), surplus
        for i in candidates:
            extra = min(reach - given[i], max(1, remaining * loads[i] // mass), surplus)
            given[i] = given[i] + extra
            surplus = surplus - extra
    return np.array(given)


def gaussian(key, extent, deviation, most, split=(), kind=jnp.bfloat16):
    drawn = deviation * jax.random.normal(key, extent, jnp.float32)
    if split:
        drawn = drawn * level_of(key, extent, split, -0.22, 0.18)
    return jnp.clip(drawn, -most, most).astype(kind)


def setup_inputs(seed: int = 0) -> dict:
    seeds = jax.random.split(jax.random.key(seed), 13)
    hidden_held = gaussian(seeds[0], (LAYERS, TOKENS, D), 1.0, 6.0, ((0, 2), (1, 8)))
    fresh_rows = gaussian(seeds[1], (TICKS - 1, TOKENS, D), 1.0, 6.0, ((1, 8),))
    doc_held = jax.vmap(lambda own: jnp.searchsorted(jnp.cumsum(uneven(own, 2 * N_EXPERT, TOKENS, TOK_DEV, 1)), jnp.arange(TOKENS), side="right"))(jax.random.split(seeds[2], LAYERS)).reshape((LAYERS, TOKENS)).astype(jnp.int32)
    doc_fresh = jax.vmap(lambda own: jnp.searchsorted(jnp.cumsum(uneven(own, 2 * N_EXPERT, TOKENS, TOK_DEV, 1)), jnp.arange(TOKENS), side="right"))(jax.random.split(seeds[3], (TICKS - 1))).reshape((TICKS - 1, TOKENS)).astype(jnp.int32)
    routes_keys = jax.random.split(jax.random.fold_in(seeds[4], 1), TICKS * LAYERS * TOKENS // TOK_DEV)
    routes_turns = jax.random.permutation(jax.random.fold_in(seeds[4], 3), TICKS * LAYERS * TOKENS // TOK_DEV)
    routes = jax.vmap(lambda own, number: shared_out(jax.random.fold_in(seeds[4], 2), own, number, TOK_DEV, EXPERTS, TOP, CAP, 2))(routes_keys, routes_turns).reshape((TICKS, LAYERS, TOKENS, TOP))
    attn_gain = jnp.clip(1.0 + 0.15 * jax.random.normal(seeds[5], (LAYERS, D), jnp.float32), 0.25, 1.75).astype(jnp.bfloat16)
    query_gain = gaussian(seeds[6], (LAYERS, D), 1.0, 4.0, ((0, 2),))
    key_gain = gaussian(seeds[7], (LAYERS, D), 1.0, 4.0, ((0, 2),))
    ffn_gain = jnp.clip(1.0 + 0.15 * jax.random.normal(seeds[8], (LAYERS, D), jnp.float32), 0.25, 1.75).astype(jnp.bfloat16)
    router = gaussian(seeds[9], (LAYERS, D, EXPERTS), D ** -0.5, 0.09375, ((0, 2),))
    weight_in = gaussian(seeds[10], (LAYERS, EXPERTS, D, 2, EXPERT_HIDDEN), D ** -0.5, 0.09375, ((0, 2), (1, 8), (4, 2)))
    weight_out = gaussian(seeds[11], (LAYERS, EXPERTS, EXPERT_HIDDEN, D), EXPERT_HIDDEN ** -0.5, 0.15625, ((0, 2), (1, 8), (2, 2)))
    return {"hidden_held": hidden_held, "fresh_rows": fresh_rows, "doc_held": doc_held, "doc_fresh": doc_fresh, "routes": routes, "attn_gain": attn_gain, "query_gain": query_gain, "key_gain": key_gain, "ffn_gain": ffn_gain, "router": router, "weight_in": weight_in, "weight_out": weight_out}


def rms_norm(rows, gain):
    wide = rows.astype(jnp.float32)
    return wide * lax.rsqrt(lax.optimization_barrier(jnp.mean(wide * wide, axis=-1, keepdims=True)) + 1e-06) * gain.astype(jnp.float32)

def attention(normed, documents, query_gain, key_gain):
    row_count = normed.shape[0]
    head_count = normed.shape[1] // HEAD_DIM
    queries = (normed.astype(jnp.float32) * query_gain.astype(jnp.float32)).astype(jnp.bfloat16)
    key_rows = (normed.astype(jnp.float32) * key_gain.astype(jnp.float32)).astype(jnp.bfloat16)

    def heads_first(rows):
        return rows.reshape(row_count, head_count, HEAD_DIM).transpose(1, 0, 2)
    places = jnp.arange(row_count, dtype=jnp.int32)
    allowed = (documents[:, None] == documents[None, :]) & (places[None, :] <= places[:, None])

    def one_head(triple):
        query_head, key_head, value_head = triple
        scores = jnp.einsum('qd,kd->qk', query_head.astype(jnp.float32), key_head.astype(jnp.float32)) * HEAD_DIM ** (-0.5)
        scores = jnp.where(allowed, scores, -1e+30)
        scores = scores - lax.optimization_barrier(jnp.max(scores, axis=1, keepdims=True))
        raised = jnp.exp(scores)
        weights = (raised / lax.optimization_barrier(jnp.sum(raised, axis=1, keepdims=True))).astype(jnp.bfloat16)
        return jnp.einsum('qk,kd->qd', weights.astype(jnp.float32), value_head.astype(jnp.float32)).astype(jnp.bfloat16)
    mixed = lax.map(one_head, (heads_first(queries), heads_first(key_rows), heads_first(normed)))
    return mixed.transpose(1, 0, 2).reshape(row_count, -1)

def expert_outputs(moe_in, chosen, weight_in, weight_out):
    labels = jnp.arange(EXPERTS, dtype=jnp.int32)
    member = lax.optimization_barrier(jnp.sum((chosen[:, :, None] == labels).astype(jnp.int32), axis=1, dtype=jnp.int32))
    ranking = jnp.cumsum(member, axis=0, dtype=jnp.int32) - member
    list_size = N_EXPERT * CAP

    def one_expert(triple):
        flags, inward, outward = triple
        picked_index = jnp.nonzero(flags > 0, size=list_size, fill_value=0)[0]
        rows = moe_in[picked_index]
        projected = jnp.dot(rows, inward.reshape(inward.shape[0], -1), preferred_element_type=jnp.float32)
        half_width = projected.shape[1] // 2
        inner_act = (jax.nn.silu(projected[:, :half_width]) * projected[:, half_width:]).astype(jnp.bfloat16)
        return jnp.dot(inner_act, outward, preferred_element_type=jnp.float32).astype(jnp.bfloat16)
    results = lax.map(one_expert, (member.T, weight_in, weight_out))
    slot_index = jnp.take_along_axis(ranking, chosen, axis=1).astype(jnp.int32)
    return results[chosen, slot_index]

def layer(current, documents, chosen, attn_gain, query_gain, key_gain, ffn_gain, router, weight_in, weight_out):
    normed = rms_norm(current, attn_gain).astype(jnp.bfloat16)
    mixed = attention(normed, documents, query_gain, key_gain)
    residual = current.astype(jnp.float32) + mixed.astype(jnp.float32)
    moe_in = rms_norm(residual, ffn_gain).astype(jnp.bfloat16)
    logits = jnp.dot(moe_in, router, preferred_element_type=jnp.float32)
    chances = jax.nn.softmax(logits, axis=-1)
    picked = jnp.take_along_axis(chances, chosen, axis=1)
    gate_weights = picked / lax.optimization_barrier(jnp.sum(picked, axis=1, keepdims=True))
    outputs = expert_outputs(moe_in, chosen, weight_in, weight_out)
    combined = lax.optimization_barrier(jnp.sum(gate_weights[:, :, None] * outputs.astype(jnp.float32), axis=1))
    return (residual + combined).astype(jnp.bfloat16)

def reference(hidden_held, fresh_rows, doc_held, doc_fresh, routes, attn_gain, query_gain, key_gain, ffn_gain, router, weight_in, weight_out):
    currents = [hidden_held[layer_index] for layer_index in range(LAYERS)]
    documents = [doc_held[layer_index] for layer_index in range(LAYERS)]
    rows_out = []
    for step_index in range(TICKS):
        made = []
        for layer_index in range(LAYERS):
            made.append(layer(currents[layer_index], documents[layer_index], routes[step_index, layer_index], attn_gain[layer_index], query_gain[layer_index], key_gain[layer_index], ffn_gain[layer_index], router[layer_index], weight_in[layer_index], weight_out[layer_index]))
        rows_out.append(jnp.stack(made))
        if step_index + 1 < TICKS:
            currents = [fresh_rows[step_index]] + made[:-1]
            documents = [doc_fresh[step_index]] + documents[:-1]
    return jnp.stack(rows_out)
```

```python
import functools

import jax
import jax.numpy as jnp
from jax import lax
from jax.experimental import pallas as pl
from jax.experimental.pallas import tpu as pltpu
from jax.sharding import PartitionSpec as P

HEAD_DIM = 128
LANES = 128
EPS = 1e-06
F32 = jnp.float32
BF16 = jnp.bfloat16
MIB = 1024 * 1024


def params(mib):
    return pltpu.CompilerParams(vmem_limit_bytes=mib * MIB)


def cost():
    return pl.CostEstimate(flops=1, bytes_accessed=1, transcendentals=0)


def vmem():
    return pl.BlockSpec(memory_space=pltpu.VMEM)


def smem():
    return pl.BlockSpec(memory_space=pltpu.SMEM)


def to_next_block(array, sections):
    count = lax.axis_size("expert")
    pairs = [(s * count + i, s * count + i + 1) for s in sections for i in range(count - 1)]
    return lax.ppermute(array, ("section", "expert"), pairs)


def to_next_phase(array, step, swap):
    count, planes = lax.axis_size("expert"), lax.axis_size("dp")
    pairs = []
    for e in range(count - step):
        for d in range(planes):
            target = (count + e + step) * planes + (planes - 1 - d if swap else d)
            pairs.append((e * planes + d, target))
    return lax.ppermute(array, ("section", "expert", "dp"), pairs)


def to_other_plane(array, sections):
    pairs = [(2 * s + d, 2 * s + 1 - d) for s in sections for d in (0, 1)]
    return lax.ppermute(array, ("section", "dp"), pairs)


def across(array, distance, sections):
    if distance == 0:
        return array
    count = lax.axis_size("expert")
    pairs = [(s * count + e, s * count + (e ^ distance)) for s in sections for e in range(count)]
    return lax.ppermute(array, ("section", "expert"), pairs)


def eye(size):
    return lax.broadcasted_iota(jnp.int32, (size, size), 0) == lax.broadcasted_iota(
        jnp.int32, (size, size), 1
    )


def as_column(row, diagonal):
    return jnp.sum(jnp.where(diagonal, row, 0.0), axis=1, keepdims=True)


def as_row(column, diagonal):
    return jnp.sum(jnp.where(diagonal, column, 0.0), axis=0, keepdims=True)


def dot(a, b, contract=((1,), (0,))):
    return lax.dot_general(a, b, (contract, ((), ())), preferred_element_type=F32)


def attend_kernel(merged, width, expert_count, scalar_ref, own_ref, prior_ref, *refs):
    meta_ref, prior_meta_ref, *refs = refs
    ids, scale = meta_ref[0:1, :], meta_ref[1:2, :]
    prior_ids, prior_scale = prior_meta_ref[0:1, :], prior_meta_ref[1:2, :]
    if merged:
        sent_ref, sent_prior_ref, ids_ref, prior_ids_ref, *refs = refs
        squares_ref, squares_other_ref, *refs = refs
        prior_squares_ref, prior_squares_other_ref, *refs = refs
        first = scalar_ref[1] == 0
        ids = jnp.where(first, ids, ids_ref[...])
        prior_ids = jnp.where(first, prior_ids, prior_ids_ref[...])
        passed = lax.rsqrt((squares_ref[...] + squares_other_ref[...]) / width + EPS)
        prior_passed = lax.rsqrt(
            (prior_squares_ref[...] + prior_squares_other_ref[...]) / width + EPS
        )
        scale = jnp.where(first, scale, passed)
        prior_scale = jnp.where(first, prior_scale, prior_passed)
    gain_ref, query_ref, key_ref, ffn_ref, router_ref, place_ref = refs[:6]
    residual_ref, stats_ref, *block_refs = refs[6:]
    rows, features = own_ref.shape
    diagonal = eye(rows)
    own_scale, prior_scale = as_column(scale, diagonal), as_column(prior_scale, diagonal)
    own_ids = as_column(ids, diagonal)
    causal = lax.broadcasted_iota(jnp.int32, (rows, rows), 1) <= lax.broadcasted_iota(
        jnp.int32, (rows, rows), 0
    )
    bias_own = jnp.where((own_ids == ids) & causal, 0.0, -1e30)
    bias_prior = jnp.where(own_ids == prior_ids, 0.0, -1e30)
    factor = HEAD_DIM ** (-0.5)
    squares = jnp.zeros((rows, HEAD_DIM), F32)
    scaled, sent_rows = [], []
    all_heads = features // HEAD_DIM
    batch = min(8, all_heads)
    for base in range(0, all_heads, batch):
        heads = [slice(h * HEAD_DIM, (h + 1) * HEAD_DIM) for h in range(base, base + batch)]
        owns, normeds, prior_normeds, scores = [], [], [], []
        for at in heads:
            gain = gain_ref[:, at].astype(F32)
            query_gain, key_gain = query_ref[:, at].astype(F32), key_ref[:, at].astype(F32)
            own, prior = own_ref[:, at], prior_ref[:, at]
            if merged:
                own = jnp.where(first, own, sent_ref[:, at])
                prior = jnp.where(first, prior, sent_prior_ref[:, at])
            own = own.astype(F32)
            normed = (own * own_scale * gain).astype(BF16)
            prior_normed = (prior.astype(F32) * prior_scale * gain).astype(BF16)
            queries = (normed.astype(F32) * query_gain).astype(BF16)
            keys = (normed.astype(F32) * key_gain).astype(BF16)
            prior_keys = (prior_normed.astype(F32) * key_gain).astype(BF16)
            owns.append(own)
            normeds.append(normed)
            prior_normeds.append(prior_normed)
            scores.append(
                (dot(queries, keys, ((1,), (1,))), dot(queries, prior_keys, ((1,), (1,))))
            )
        weights = []
        for score, prior_score in scores:
            score = score * factor + bias_own
            prior_score = prior_score * factor + bias_prior
            top = jnp.max(jnp.maximum(score, prior_score), axis=1, keepdims=True)
            raised, prior_raised = jnp.exp(score - top), jnp.exp(prior_score - top)
            inverse = 1.0 / jnp.sum(raised + prior_raised, axis=1, keepdims=True)
            weights.append(
                ((raised * inverse).astype(BF16), (prior_raised * inverse).astype(BF16))
            )
        for index, at in enumerate(heads):
            weight, prior_weight = weights[index]
            mixed = dot(weight, normeds[index]) + dot(prior_weight, prior_normeds[index])
            residual = owns[index] + mixed.astype(BF16).astype(F32)
            residual_ref[:, at] = residual
            squares = squares + residual * residual
            scaled.append((residual * ffn_ref[:, at].astype(F32)).astype(BF16))
            sent_rows.append(residual.astype(BF16))
    sent = dot(place_ref[...], jnp.concatenate(sent_rows, axis=1)).astype(BF16)
    start = 0
    for block_ref in block_refs:
        block_ref[...] = sent[start : start + block_ref.shape[0]]
        start += block_ref.shape[0]
    squares = jnp.sum(squares, axis=1, keepdims=True)
    logits = dot(jnp.concatenate(scaled, axis=1), router_ref[...], ((1,), (1,)))
    lane = lax.broadcasted_iota(jnp.int32, (rows, LANES), 1)
    stats_ref[...] = jnp.where(lane == expert_count, squares, logits)


def attend(merged, width, expert_count, plane, operands, gains, router, place):
    rows, features = operands[0].shape
    capacity = place.shape[0] // expert_count
    whole = lambda shape: pl.BlockSpec(shape, lambda step, plane_ref: (0, 0))
    side = lambda step, plane_ref: (0, plane_ref[0])
    in_specs = [whole(array.shape) for array in operands]
    in_specs += [pl.BlockSpec((1, features), side)] * len(gains)
    in_specs += [pl.BlockSpec((LANES, features), side), whole(place.shape)]
    shapes = [((rows, features), F32), ((rows, LANES), F32)]
    shapes += [((capacity, features), BF16)] * expert_count
    residual, stats, *blocks = pl.pallas_call(
        functools.partial(attend_kernel, merged, width, expert_count),
        out_shape=[jax.ShapeDtypeStruct(*shape) for shape in shapes],
        grid_spec=pltpu.PrefetchScalarGridSpec(
            num_scalar_prefetch=1,
            grid=(1,),
            in_specs=in_specs,
            out_specs=[whole(shape) for shape, _ in shapes],
        ),
        compiler_params=params(16),
        cost_estimate=cost(),
        name="attend",
    )(plane, *operands, *gains, router, place)
    return residual, stats, blocks


def expert_kernel(blocks, width, scalar_ref, *refs):
    own_refs, far_refs, refs = refs[:blocks], refs[blocks : 2 * blocks], refs[2 * blocks :]
    up_ref, down_ref, gain_ref, *refs = refs
    away_refs, kept_refs = refs[:blocks], refs[blocks : 2 * blocks]
    rows_ref, sum_ref, inner_ref, up_held, down_held, up_sems, down_sems = refs[2 * blocks :]
    slots, half = rows_ref.shape[1:]
    hidden = down_ref.shape[0]
    plane = scalar_ref[0]
    sides = (plane * half, (1 - plane) * half)
    depth = up_held.shape[1]
    parts = half // depth
    down_depth = down_held.shape[1]

    copies = []
    for index in range(2 * parts):
        first = pl.multiple_of(sides[index // parts] + index % parts * depth, depth)
        copies.append(
            pltpu.make_async_copy(
                up_ref.at[pl.ds(first, depth)], up_held.at[index], up_sems.at[index]
            )
        )
    down_copies = [
        pltpu.make_async_copy(
            down_ref.at[pl.ds(index * down_depth, down_depth)],
            down_held.at[index],
            down_sems.at[index],
        )
        for index in range(hidden // down_depth)
    ]
    for copy in copies + down_copies:
        copy.start()

    scales = []
    start = 0
    for own_ref, far_ref in zip(own_refs, far_refs):
        at = slice(start, start + own_ref.shape[0])
        start += own_ref.shape[0]
        squares = 0.0
        for which, source_ref in enumerate((own_ref, far_ref)):
            lanes = pl.ds(pl.multiple_of(sides[which], half), half)
            rows = source_ref[...].astype(F32)
            squares = squares + jnp.sum(rows * rows, axis=1, keepdims=True)
            rows_ref[which, at, :] = (rows * gain_ref[:, lanes].astype(F32)).astype(BF16)
        scales.append(lax.rsqrt(squares / width + EPS))
    scale = jnp.concatenate(scales, axis=0)

    columns = min(512, hidden)
    for index, copy in enumerate(copies):
        copy.wait()
        lanes = slice(index % parts * depth, (index % parts + 1) * depth)

        @pl.loop(0, 2 * hidden // columns)
        def _(step, index=index, lanes=lanes):
            at = pl.ds(pl.multiple_of(step * columns, columns), columns)
            made = dot(rows_ref[index // parts, :, lanes], up_held[index, :, at])
            sum_ref[:, at] = made if index == 0 else sum_ref[:, at] + made

    gate = sum_ref[:, :hidden] * scale
    value = sum_ref[:, hidden:] * scale
    inner_ref[...] = (gate / (1.0 + jnp.exp(-gate)) * value).astype(BF16)
    for copy in down_copies:
        copy.wait()
    columns = min(512, half)
    for target_refs, side in ((away_refs, sides[1]), (kept_refs, sides[0])):

        @pl.loop(0, half // columns)
        def _(step, target_refs=target_refs, side=side):
            first = pl.multiple_of(step * columns, columns)
            at = pl.ds(pl.multiple_of(side + first, columns), columns)
            made = 0.0
            for index in range(hidden // down_depth):
                inner = inner_ref[:, index * down_depth : (index + 1) * down_depth]
                made = made + dot(inner, down_held[index, :, at])
            start = 0
            for ref in target_refs:
                piece = made[start : start + ref.shape[0]]
                ref[:, pl.ds(first, columns)] = piece.astype(ref.dtype)
                start += ref.shape[0]


def expert_rows(scalars, own, far, up, down, gain):
    blocks = len(own)
    slots = sum(array.shape[0] for array in own)
    half = own[0].shape[1]
    hidden, width = down.shape
    depth, down_depth = min(1024, half), min(256, hidden)
    anywhere = pl.BlockSpec(memory_space=pl.ANY)
    outs = pl.pallas_call(
        functools.partial(expert_kernel, blocks, width),
        out_shape=[jax.ShapeDtypeStruct(array.shape, BF16) for array in (*own, *own)],
        in_specs=[smem()] + [vmem()] * (2 * blocks) + [anywhere, anywhere, vmem()],
        out_specs=[vmem()] * (2 * blocks),
        scratch_shapes=[
            pltpu.VMEM((2, slots, half), BF16),
            pltpu.VMEM((slots, 2 * hidden), F32),
            pltpu.VMEM((slots, hidden), BF16),
            pltpu.VMEM((width // depth, depth, 2 * hidden), BF16),
            pltpu.VMEM((hidden // down_depth, down_depth, width), BF16),
            pltpu.SemaphoreType.DMA((width // depth,)),
            pltpu.SemaphoreType.DMA((hidden // down_depth,)),
        ],
        compiler_params=params(32),
        cost_estimate=cost(),
        name="expert_rows",
    )(scalars, *own, *far, up, down, gain)
    return list(outs[:blocks]), list(outs[blocks:])


def combine_kernel(expert_count, width, *refs):
    *rows_refs, residual_ref, stats_ref, stats_other_ref, place_ref, made_ref, squares_ref = refs
    tokens, slots = place_ref.shape
    capacity = slots // expert_count
    stats = stats_ref[...] + stats_other_ref[...]
    lane = lax.broadcasted_iota(jnp.int32, (tokens, LANES), 1)
    total = jnp.sum(jnp.where(lane == expert_count, stats, 0.0), axis=1, keepdims=True)
    logits = stats * lax.rsqrt(total / width + EPS)
    expert = lax.broadcasted_iota(jnp.int32, (LANES, slots), 0)
    slot = lax.broadcasted_iota(jnp.int32, (LANES, slots), 1)
    spread = jnp.where(
        (slot >= expert * capacity) & (slot < (expert + 1) * capacity), 1.0, 0.0
    ).astype(BF16)
    place = place_ref[...]
    member = dot(place, spread, ((1,), (1,))) > 0.5
    logits = jnp.where(member, logits, -1e30)
    raised = jnp.exp(logits - jnp.max(logits, axis=1, keepdims=True))
    gates = raised / jnp.sum(raised, axis=1, keepdims=True)
    high = gates.astype(BF16)
    low = (gates - high.astype(F32)).astype(BF16)
    place = place.astype(F32)
    rows = jnp.concatenate([ref[...] for ref in rows_refs], axis=0)
    made = dot((dot(high, spread) * place).astype(BF16), rows)
    made = made + dot((dot(low, spread) * place).astype(BF16), rows)
    made = (residual_ref[...] + made).astype(BF16)
    made_ref[...] = made
    wide = made.astype(F32)
    squares_ref[...] = as_row(jnp.sum(wide * wide, axis=1, keepdims=True), eye(tokens))


def combine(expert_count, width, returned, residual, stats, stats_other, place):
    tokens, features = residual.shape
    return pl.pallas_call(
        functools.partial(combine_kernel, expert_count, width),
        out_shape=(
            jax.ShapeDtypeStruct((tokens, features), BF16),
            jax.ShapeDtypeStruct((1, tokens), F32),
        ),
        in_specs=[vmem()] * (len(returned) + 4),
        out_specs=(vmem(), vmem()),
        compiler_params=params(16),
        cost_estimate=cost(),
        name="combine",
    )(*returned, residual, stats, stats_other, place)


def body(
    hidden_held,
    fresh_rows,
    doc_held,
    doc_fresh,
    routes,
    attn_gain,
    query_gain,
    key_gain,
    ffn_gain,
    router,
    weight_in,
    weight_out,
):
    ticks = routes.shape[0]
    assert ticks == 2 and lax.axis_size("section") == 2 and lax.axis_size("dp") == 2
    tokens, width = hidden_held.shape[1:]
    top_count = routes.shape[3]
    count = router.shape[2]
    assert count == lax.axis_size("expert")
    capacity = min(tokens, 3 * tokens * top_count // (2 * count))
    capacity = -(-capacity // 16) * 16
    section = lax.axis_index("section").astype(jnp.int32)
    plane = lax.axis_index("dp").astype(jnp.int32)
    here = lax.axis_index("expert").astype(jnp.int32)
    half = width // 2
    scalars = jnp.stack([plane, section])
    both = (0, 1)

    def half_of(rows):
        return lax.dynamic_slice_in_dim(rows, plane * half, half, 1)

    def meta_of(rows, ids):
        wide = rows.astype(F32)
        scale = lax.rsqrt(jnp.mean(wide * wide, axis=1) + EPS)
        return jnp.stack([(ids + 1).astype(F32), scale])

    held = half_of(hidden_held[0])
    held_prior = to_next_block(held, both)
    held_meta = meta_of(hidden_held[0], doc_held[0])
    held_prior_meta = to_next_block(held_meta, both)

    labels = jnp.arange(count, dtype=jnp.int32)
    gains = [attn_gain, query_gain, key_gain, ffn_gain]
    wanted = (jnp.arange(LANES, dtype=jnp.int32)[:, None] == (labels ^ here)[None, :]).astype(BF16)
    router_rows = jnp.dot(wanted, router[0].T, preferred_element_type=F32).astype(BF16)
    up_weight = weight_in[0, 0].reshape(width, -1)
    down_weight = weight_out[0, 0]

    chosen = routes[:, 0] ^ here
    member = jnp.sum((chosen[..., None] == labels).astype(F32), axis=2)
    before = jnp.tril(jnp.ones((tokens, tokens), F32), -1)
    ranking = jnp.einsum("ij,tje->tie", before, member).astype(jnp.int32)
    ranking = jnp.where(member > 0, ranking, -1)
    slot = jnp.arange(capacity, dtype=jnp.int32)
    combine_place = (ranking[:, :, :, None] == slot).astype(BF16)
    combine_place = combine_place.reshape(ticks, tokens, count * capacity)
    send_place = (ranking.transpose(0, 2, 1)[:, :, None, :] == slot[:, None]).astype(BF16)
    send_place = send_place.reshape(ticks, count * capacity, tokens)

    near = range(count // 2)
    far, farther = range(count // 2, 3 * count // 4), range(3 * count // 4, count)

    def exchange(blocks):
        got = list(blocks)
        for k in [*far, *near]:
            got[k] = across(blocks[k], k, both)
        for k, sooner in zip(farther, far):
            block, got[sooner] = lax.optimization_barrier((blocks[k], got[sooner]))
            got[k] = across(block, k, both)
        return got

    def experts(own):
        other = [to_other_plane(block, both) for block in own]
        away, kept = [], []
        for group in ([*near, *far], farther):
            mine, theirs = [own[k] for k in group], [other[k] for k in group]
            if kept:
                theirs[0], kept[0] = lax.optimization_barrier((theirs[0], kept[0]))
            made = expert_rows(scalars, mine, theirs, up_weight, down_weight, ffn_gain)
            away += made[0]
            kept += made[1]
        received = [None] * count
        for k in [*far, *farther]:
            received[k] = to_other_plane(away[k], both)
        for k in near:
            later = far[k % len(far)]
            block, received[later] = lax.optimization_barrier((away[k], received[later]))
            received[k] = to_other_plane(block, both)
        return [k + r for k, r in zip(kept, received)]

    def whole_rows(made):
        other = to_other_plane(made, both)
        low, high = jnp.where(plane == 0, made, other), jnp.where(plane == 0, other, made)
        return jnp.concatenate([low, high], axis=1)

    ids = held_meta[0:1]
    sent_ids = [to_next_phase(ids, step, False) for step in (0, 1)]
    held_meta, up_weight, *sent_ids = lax.optimization_barrier((held_meta, up_weight, *sent_ids))
    residual, stats, rows = attend(
        False, width, count, scalars, [held, held_prior, held_meta, held_prior_meta],
        gains, router_rows, send_place[0],
    )
    stats_other = to_other_plane(stats, both)
    returned = exchange(experts(exchange(rows)))
    made, squares = combine(
        count, width, returned, residual, stats, stats_other, combine_place[0]
    )

    fresh = half_of(fresh_rows[0])
    fresh_prior = to_next_block(fresh, (0,))
    fresh_meta = meta_of(fresh_rows[0], doc_fresh[0])
    fresh_prior_meta = to_next_block(fresh_meta, (0,))
    sent_prior, sent = to_next_phase(made, 1, False), to_next_phase(made, 0, False)
    scales = [to_next_phase(squares, step, swap) for step in (0, 1) for swap in (False, True)]
    results = [whole_rows(made)]
    residual, stats, rows = attend(
        True, width, count, scalars,
        [fresh, fresh_prior, fresh_meta, fresh_prior_meta, sent, sent_prior, *sent_ids, *scales],
        gains, router_rows, send_place[1],
    )
    stats_other = to_other_plane(stats, both)
    returned = exchange(experts(exchange(rows)))
    made, squares = combine(
        count, width, returned, residual, stats, stats_other, combine_place[1]
    )
    results.append(whole_rows(made))
    return jnp.stack(results)[:, None]


def solution(mesh):
    in_specs = (
        P("section", "expert", None),
        P(None, "expert", None),
        P("section", "expert"),
        P(None, "expert"),
        P(None, "section", "expert", None),
        P("section", None),
        P("section", None),
        P("section", None),
        P("section", None),
        P("section", None, None),
        P("section", "expert", None, None, "dp"),
        P("section", "expert", "dp", None),
    )
    out_specs = P(None, "section", "expert", None)
    return jax.shard_map(body, mesh=mesh, in_specs=in_specs, out_specs=out_specs, check_vma=False)
```

```python
import functools

import jax
import jax.numpy as jnp
from jax import lax
from jax.experimental import pallas as pl
from jax.experimental.pallas import tpu as pltpu
from jax.sharding import PartitionSpec as P

HEAD_DIM = 128
LANES = 128
EPS = 1e-06
F32 = jnp.float32
BF16 = jnp.bfloat16
MIB = 1024 * 1024
IN_FLIGHT = 4


def params(mib):
    return pltpu.CompilerParams(vmem_limit_bytes=mib * MIB)


def cost():
    return pl.CostEstimate(flops=1, bytes_accessed=1, transcendentals=0)


def vmem():
    return pl.BlockSpec(memory_space=pltpu.VMEM)


def smem():
    return pl.BlockSpec(memory_space=pltpu.SMEM)


def to_next_block(array, sections):
    count = lax.axis_size("expert")
    pairs = [(s * count + i, s * count + i + 1) for s in sections for i in range(count - 1)]
    return lax.ppermute(array, ("section", "expert"), pairs)


def to_next_phase(array, step, swap):
    count, planes = lax.axis_size("expert"), lax.axis_size("dp")
    pairs = []
    for e in range(count - step):
        for d in range(planes):
            target = (count + e + step) * planes + (planes - 1 - d if swap else d)
            pairs.append((e * planes + d, target))
    return lax.ppermute(array, ("section", "expert", "dp"), pairs)


def to_other_plane(array, sections):
    pairs = [(2 * s + d, 2 * s + 1 - d) for s in sections for d in (0, 1)]
    return lax.ppermute(array, ("section", "dp"), pairs)


def across(array, distance, sections):
    if distance == 0:
        return array
    count = lax.axis_size("expert")
    pairs = [(s * count + e, s * count + (e ^ distance)) for s in sections for e in range(count)]
    return lax.ppermute(array, ("section", "expert"), pairs)


def eye(size):
    return lax.broadcasted_iota(jnp.int32, (size, size), 0) == lax.broadcasted_iota(
        jnp.int32, (size, size), 1
    )


def as_column(row, diagonal):
    return jnp.sum(jnp.where(diagonal, row, 0.0), axis=1, keepdims=True)


def as_row(column, diagonal):
    return jnp.sum(jnp.where(diagonal, column, 0.0), axis=0, keepdims=True)


def dot(a, b, contract=((1,), (0,))):
    return lax.dot_general(a, b, (contract, ((), ())), preferred_element_type=F32)


def attend_kernel(merged, width, expert_count, scalar_ref, own_ref, prior_ref, *refs):
    meta_ref, prior_meta_ref, *refs = refs
    ids, scale = meta_ref[0:1, :], meta_ref[1:2, :]
    prior_ids, prior_scale = prior_meta_ref[0:1, :], prior_meta_ref[1:2, :]
    if merged:
        sent_ref, sent_prior_ref, ids_ref, prior_ids_ref, *refs = refs
        squares_ref, squares_other_ref, *refs = refs
        prior_squares_ref, prior_squares_other_ref, *refs = refs
        first = scalar_ref[1] == 0
        ids = jnp.where(first, ids, ids_ref[...])
        prior_ids = jnp.where(first, prior_ids, prior_ids_ref[...])
        passed = lax.rsqrt((squares_ref[...] + squares_other_ref[...]) / width + EPS)
        prior_passed = lax.rsqrt(
            (prior_squares_ref[...] + prior_squares_other_ref[...]) / width + EPS
        )
        scale = jnp.where(first, scale, passed)
        prior_scale = jnp.where(first, prior_scale, prior_passed)
    gain_ref, query_ref, key_ref, ffn_ref, router_ref, place_ref = refs[:6]
    residual_ref, stats_ref, *block_refs = refs[6:]
    rows, features = own_ref.shape
    diagonal = eye(rows)
    own_scale, prior_scale = as_column(scale, diagonal), as_column(prior_scale, diagonal)
    own_ids = as_column(ids, diagonal)
    causal = lax.broadcasted_iota(jnp.int32, (rows, rows), 1) <= lax.broadcasted_iota(
        jnp.int32, (rows, rows), 0
    )
    bias_own = jnp.where((own_ids == ids) & causal, 0.0, -1e30)
    bias_prior = jnp.where(own_ids == prior_ids, 0.0, -1e30)
    factor = HEAD_DIM ** (-0.5)
    squares = jnp.zeros((rows, HEAD_DIM), F32)
    scaled, sent_rows = [], []
    all_heads = features // HEAD_DIM
    batch = min(8, all_heads)
    for base in range(0, all_heads, batch):
        heads = [slice(h * HEAD_DIM, (h + 1) * HEAD_DIM) for h in range(base, base + batch)]
        owns, normeds, prior_normeds, scores = [], [], [], []
        for at in heads:
            gain = gain_ref[:, at].astype(F32)
            query_gain, key_gain = query_ref[:, at].astype(F32), key_ref[:, at].astype(F32)
            own, prior = own_ref[:, at], prior_ref[:, at]
            if merged:
                own = jnp.where(first, own, sent_ref[:, at])
                prior = jnp.where(first, prior, sent_prior_ref[:, at])
            own = own.astype(F32)
            normed = (own * own_scale * gain).astype(BF16)
            prior_normed = (prior.astype(F32) * prior_scale * gain).astype(BF16)
            queries = (normed.astype(F32) * query_gain).astype(BF16)
            keys = (normed.astype(F32) * key_gain).astype(BF16)
            prior_keys = (prior_normed.astype(F32) * key_gain).astype(BF16)
            owns.append(own)
            normeds.append(normed)
            prior_normeds.append(prior_normed)
            scores.append(
                (dot(queries, keys, ((1,), (1,))), dot(queries, prior_keys, ((1,), (1,))))
            )
        weights = []
        for score, prior_score in scores:
            score = score * factor + bias_own
            prior_score = prior_score * factor + bias_prior
            top = jnp.max(jnp.maximum(score, prior_score), axis=1, keepdims=True)
            raised, prior_raised = jnp.exp(score - top), jnp.exp(prior_score - top)
            inverse = 1.0 / jnp.sum(raised + prior_raised, axis=1, keepdims=True)
            weights.append(
                ((raised * inverse).astype(BF16), (prior_raised * inverse).astype(BF16))
            )
        for index, at in enumerate(heads):
            weight, prior_weight = weights[index]
            mixed = dot(weight, normeds[index]) + dot(prior_weight, prior_normeds[index])
            residual = owns[index] + mixed.astype(BF16).astype(F32)
            residual_ref[:, at] = residual
            squares = squares + residual * residual
            scaled.append((residual * ffn_ref[:, at].astype(F32)).astype(BF16))
            sent_rows.append(residual.astype(BF16))
    sent = dot(place_ref[...], jnp.concatenate(sent_rows, axis=1)).astype(BF16)
    start = 0
    for block_ref in block_refs:
        block_ref[...] = sent[start : start + block_ref.shape[0]]
        start += block_ref.shape[0]
    squares = jnp.sum(squares, axis=1, keepdims=True)
    logits = dot(jnp.concatenate(scaled, axis=1), router_ref[...], ((1,), (1,)))
    lane = lax.broadcasted_iota(jnp.int32, (rows, LANES), 1)
    stats_ref[...] = jnp.where(lane == expert_count, squares, logits)


def attend(merged, width, expert_count, plane, operands, gains, router, place):
    rows, features = operands[0].shape
    capacity = place.shape[0] // expert_count
    whole = lambda shape: pl.BlockSpec(shape, lambda step, plane_ref: (0, 0))
    side = lambda step, plane_ref: (0, plane_ref[0])
    in_specs = [whole(array.shape) for array in operands]
    in_specs += [pl.BlockSpec((1, features), side)] * len(gains)
    in_specs += [pl.BlockSpec((LANES, features), side), whole(place.shape)]
    shapes = [((rows, features), F32), ((rows, LANES), F32)]
    shapes += [((capacity, features), BF16)] * expert_count
    residual, stats, *blocks = pl.pallas_call(
        functools.partial(attend_kernel, merged, width, expert_count),
        out_shape=[jax.ShapeDtypeStruct(*shape) for shape in shapes],
        grid_spec=pltpu.PrefetchScalarGridSpec(
            num_scalar_prefetch=1,
            grid=(1,),
            in_specs=in_specs,
            out_specs=[whole(shape) for shape, _ in shapes],
        ),
        compiler_params=params(16),
        cost_estimate=cost(),
        name="attend",
    )(plane, *operands, *gains, router, place)
    return residual, stats, blocks


def expert_kernel(blocks, groups, width, scalar_ref, *refs):
    own_refs, far_refs, refs = refs[:blocks], refs[blocks : 2 * blocks], refs[2 * blocks :]
    up_ref, down_ref, gain_ref, *refs = refs
    away_refs, kept_refs = refs[:groups], refs[groups : 2 * groups]
    rows_ref, sum_ref, inner_ref, up_held, down_held, up_sems, down_sems = refs[2 * groups :]
    slots, half = rows_ref.shape[1:]
    hidden = down_ref.shape[0]
    plane = scalar_ref[0]
    sides = (plane * half, (1 - plane) * half)
    depth = up_held.shape[1]
    parts = half // depth
    down_depth = down_held.shape[1]

    copies = []
    for index in range(2 * parts):
        first = pl.multiple_of(sides[index // parts] + index % parts * depth, depth)
        copies.append(
            pltpu.make_async_copy(
                up_ref.at[pl.ds(first, depth)], up_held.at[index], up_sems.at[index]
            )
        )
    down_copies = [
        pltpu.make_async_copy(
            down_ref.at[pl.ds(index * down_depth, down_depth)],
            down_held.at[index],
            down_sems.at[index],
        )
        for index in range(hidden // down_depth)
    ]
    order = copies + down_copies
    for copy in order[:IN_FLIGHT]:
        copy.start()

    def landed(index):
        order[index].wait()
        if index + IN_FLIGHT < len(order):
            order[index + IN_FLIGHT].start()

    scales = []
    start = 0
    for own_ref, far_ref in zip(own_refs, far_refs):
        at = slice(start, start + own_ref.shape[0])
        start += own_ref.shape[0]
        squares = 0.0
        for which, source_ref in enumerate((own_ref, far_ref)):
            lanes = pl.ds(pl.multiple_of(sides[which], half), half)
            rows = source_ref[...].astype(F32)
            squares = squares + jnp.sum(rows * rows, axis=1, keepdims=True)
            rows_ref[which, at, :] = (rows * gain_ref[:, lanes].astype(F32)).astype(BF16)
        scales.append(lax.rsqrt(squares / width + EPS))
    scale = jnp.concatenate(scales, axis=0)

    columns = min(512, hidden)
    for index in range(len(copies)):
        landed(index)
        lanes = slice(index % parts * depth, (index % parts + 1) * depth)

        @pl.loop(0, 2 * hidden // columns)
        def _(step, index=index, lanes=lanes):
            at = pl.ds(pl.multiple_of(step * columns, columns), columns)
            made = dot(rows_ref[index // parts, :, lanes], up_held[index, :, at])
            sum_ref[:, at] = made if index == 0 else sum_ref[:, at] + made

    gate = sum_ref[:, :hidden] * scale
    value = sum_ref[:, hidden:] * scale
    inner_ref[...] = (gate / (1.0 + jnp.exp(-gate)) * value).astype(BF16)
    for index in range(len(copies), len(order)):
        landed(index)
    columns = min(512, half)
    for target_refs, side in ((away_refs, sides[1]), (kept_refs, sides[0])):

        @pl.loop(0, half // columns)
        def _(step, target_refs=target_refs, side=side):
            first = pl.multiple_of(step * columns, columns)
            at = pl.ds(pl.multiple_of(side + first, columns), columns)
            made = 0.0
            for index in range(hidden // down_depth):
                inner = inner_ref[:, index * down_depth : (index + 1) * down_depth]
                made = made + dot(inner, down_held[index, :, at])
            start = 0
            for ref in target_refs:
                piece = made[start : start + ref.shape[0]]
                ref[:, pl.ds(first, columns)] = piece.astype(ref.dtype)
                start += ref.shape[0]


def expert_rows(scalars, own, far, sizes, up, down, gain):
    blocks = len(own)
    slots = sum(array.shape[0] for array in own)
    half = own[0].shape[1]
    hidden, width = down.shape
    groups = [jax.ShapeDtypeStruct((size * own[0].shape[0], half), BF16) for size in sizes]
    depth, down_depth = min(1024, half), min(256, hidden)
    anywhere = pl.BlockSpec(memory_space=pl.ANY)
    outs = pl.pallas_call(
        functools.partial(expert_kernel, blocks, len(groups), width),
        out_shape=groups + groups,
        in_specs=[smem()] + [vmem()] * (2 * blocks) + [anywhere, anywhere, vmem()],
        out_specs=[vmem()] * (2 * len(groups)),
        scratch_shapes=[
            pltpu.VMEM((2, slots, half), BF16),
            pltpu.VMEM((slots, 2 * hidden), F32),
            pltpu.VMEM((slots, hidden), BF16),
            pltpu.VMEM((width // depth, depth, 2 * hidden), BF16),
            pltpu.VMEM((hidden // down_depth, down_depth, width), BF16),
            pltpu.SemaphoreType.DMA((width // depth,)),
            pltpu.SemaphoreType.DMA((hidden // down_depth,)),
        ],
        compiler_params=params(32),
        cost_estimate=cost(),
        name="expert_rows",
    )(scalars, *own, *far, up, down, gain)
    return outs[: len(groups)], outs[len(groups) :]


def combine_kernel(expert_count, width, *refs):
    *rows_refs, residual_ref, stats_ref, stats_other_ref, place_ref, made_ref, squares_ref = refs
    tokens, slots = place_ref.shape
    capacity = slots // expert_count
    stats = stats_ref[...] + stats_other_ref[...]
    lane = lax.broadcasted_iota(jnp.int32, (tokens, LANES), 1)
    total = jnp.sum(jnp.where(lane == expert_count, stats, 0.0), axis=1, keepdims=True)
    logits = stats * lax.rsqrt(total / width + EPS)
    expert = lax.broadcasted_iota(jnp.int32, (LANES, slots), 0)
    slot = lax.broadcasted_iota(jnp.int32, (LANES, slots), 1)
    spread = jnp.where(
        (slot >= expert * capacity) & (slot < (expert + 1) * capacity), 1.0, 0.0
    ).astype(BF16)
    place = place_ref[...]
    member = dot(place, spread, ((1,), (1,))) > 0.5
    logits = jnp.where(member, logits, -1e30)
    raised = jnp.exp(logits - jnp.max(logits, axis=1, keepdims=True))
    gates = raised / jnp.sum(raised, axis=1, keepdims=True)
    high = gates.astype(BF16)
    low = (gates - high.astype(F32)).astype(BF16)
    place = place.astype(F32)
    rows = jnp.concatenate([ref[...] for ref in rows_refs], axis=0)
    made = dot((dot(high, spread) * place).astype(BF16), rows)
    made = made + dot((dot(low, spread) * place).astype(BF16), rows)
    made = (residual_ref[...] + made).astype(BF16)
    made_ref[...] = made
    wide = made.astype(F32)
    squares_ref[...] = as_row(jnp.sum(wide * wide, axis=1, keepdims=True), eye(tokens))


def combine(expert_count, width, returned, residual, stats, stats_other, place):
    tokens, features = residual.shape
    return pl.pallas_call(
        functools.partial(combine_kernel, expert_count, width),
        out_shape=(
            jax.ShapeDtypeStruct((tokens, features), BF16),
            jax.ShapeDtypeStruct((1, tokens), F32),
        ),
        in_specs=[vmem()] * (len(returned) + 4),
        out_specs=(vmem(), vmem()),
        compiler_params=params(16),
        cost_estimate=cost(),
        name="combine",
    )(*returned, residual, stats, stats_other, place)


def body(
    hidden_held,
    fresh_rows,
    doc_held,
    doc_fresh,
    routes,
    attn_gain,
    query_gain,
    key_gain,
    ffn_gain,
    router,
    weight_in,
    weight_out,
):
    ticks = routes.shape[0]
    assert ticks == 2 and lax.axis_size("section") == 2 and lax.axis_size("dp") == 2
    tokens, width = hidden_held.shape[1:]
    top_count = routes.shape[3]
    count = router.shape[2]
    assert count == lax.axis_size("expert")
    capacity = min(tokens, 3 * tokens * top_count // (2 * count))
    capacity = -(-capacity // 16) * 16
    section = lax.axis_index("section").astype(jnp.int32)
    plane = lax.axis_index("dp").astype(jnp.int32)
    here = lax.axis_index("expert").astype(jnp.int32)
    half = width // 2
    scalars = jnp.stack([plane, section])
    both = (0, 1)

    def half_of(rows):
        return lax.dynamic_slice_in_dim(rows, plane * half, half, 1)

    def meta_of(rows, ids):
        wide = rows.astype(F32)
        scale = lax.rsqrt(jnp.mean(wide * wide, axis=1) + EPS)
        return jnp.stack([(ids + 1).astype(F32), scale])

    held = half_of(hidden_held[0])
    held_prior = to_next_block(held, both)
    held_meta = meta_of(hidden_held[0], doc_held[0])
    held_prior_meta = to_next_block(held_meta, both)

    labels = jnp.arange(count, dtype=jnp.int32)
    gains = [attn_gain, query_gain, key_gain, ffn_gain]
    wanted = (jnp.arange(LANES, dtype=jnp.int32)[:, None] == (labels ^ here)[None, :]).astype(BF16)
    router_rows = jnp.dot(wanted, router[0].T, preferred_element_type=F32).astype(BF16)
    up_weight = weight_in[0, 0].reshape(width, -1)
    down_weight = weight_out[0, 0]

    chosen = routes[:, 0] ^ here
    member = jnp.sum((chosen[..., None] == labels).astype(F32), axis=2)
    before = jnp.tril(jnp.ones((tokens, tokens), F32), -1)
    ranking = jnp.einsum("ij,tje->tie", before, member).astype(jnp.int32)
    ranking = jnp.where(member > 0, ranking, -1)
    slot = jnp.arange(capacity, dtype=jnp.int32)
    combine_place = (ranking[:, :, :, None] == slot).astype(BF16)
    combine_place = combine_place.reshape(ticks, tokens, count * capacity)
    send_place = (ranking.transpose(0, 2, 1)[:, :, None, :] == slot[:, None]).astype(BF16)
    send_place = send_place.reshape(ticks, count * capacity, tokens)

    near = range(count // 2)
    far, farther = range(count // 2, 3 * count // 4), range(3 * count // 4, count)

    def dispatch(blocks, *sooner):
        got = list(blocks)
        for k in [*far, *near]:
            got[k] = across(blocks[k], k, both)
        first = [to_other_plane(got[k], both) for k in (0, 1)]
        held, first, sooner = lax.optimization_barrier(([got[k] for k in far], first, sooner))
        for k, block in zip(far, held):
            got[k] = block
        for k, earlier in zip(farther, far):
            block, got[earlier] = lax.optimization_barrier((blocks[k], got[earlier]))
            got[k] = across(block, k, both)
        return got, first + [to_other_plane(block, both) for block in got[2:]], sooner

    def answer(own, other):
        parts = (near, far, farther)
        sizes = [len(part) for part in parts]
        away, kept = expert_rows(scalars, own, other, sizes, up_weight, down_weight, ffn_gain)
        received = [None, to_other_plane(away[1], both), to_other_plane(away[2], both)]
        rows, received[1] = lax.optimization_barrier((away[0], received[1]))
        received[0] = to_other_plane(rows, both)
        got = [None] * count
        for index in (1, 2, 0):
            for place, k in enumerate(parts[index]):
                at = slice(place * capacity, (place + 1) * capacity)
                got[k] = across(kept[index][at] + received[index][at], k, both)
        return got

    def whole_rows(made, other):
        low, high = jnp.where(plane == 0, made, other), jnp.where(plane == 0, other, made)
        return jnp.concatenate([low, high], axis=1)

    ids = held_meta[0:1]
    sent_ids = [to_next_phase(ids, step, False) for step in (0, 1)]
    held_meta, up_weight, *sent_ids = lax.optimization_barrier((held_meta, up_weight, *sent_ids))
    residual, stats, rows = attend(
        False, width, count, scalars, [held, held_prior, held_meta, held_prior_meta],
        gains, router_rows, send_place[0],
    )
    stats_other = to_other_plane(stats, both)
    own, other, _ = dispatch(rows)
    own[0], fresh_rows, doc_fresh = lax.optimization_barrier((own[0], fresh_rows, doc_fresh))
    fresh = half_of(fresh_rows[0])
    fresh_prior = to_next_block(fresh, (0,))
    fresh_meta = meta_of(fresh_rows[0], doc_fresh[0])
    fresh_prior_meta = to_next_block(fresh_meta, (0,))
    returned = answer(own, other)
    last = count - 1
    returned[last], fresh_prior, fresh_prior_meta = lax.optimization_barrier(
        (returned[last], fresh_prior, fresh_prior_meta)
    )
    made, squares = combine(
        count, width, returned, residual, stats, stats_other, combine_place[0]
    )

    sent_prior, sent = to_next_phase(made, 1, False), to_next_phase(made, 0, False)
    scales = [to_next_phase(squares, step, swap) for step in (0, 1) for swap in (False, True)]
    other = to_other_plane(made, both)
    sent, other = lax.optimization_barrier((sent, other))
    results = [whole_rows(made, other)]
    residual, stats, rows = attend(
        True, width, count, scalars,
        [fresh, fresh_prior, fresh_meta, fresh_prior_meta, sent, sent_prior, *sent_ids, *scales],
        gains, router_rows, send_place[1],
    )
    stats_other = to_other_plane(stats, both)
    own, other, _ = dispatch(rows)
    returned = answer(own, other)
    made, squares = combine(
        count, width, returned, residual, stats, stats_other, combine_place[1]
    )
    results.append(whole_rows(made, to_other_plane(made, both)))
    return jnp.stack(results)[:, None]


def solution(mesh):
    in_specs = (
        P("section", "expert", None),
        P(None, "expert", None),
        P("section", "expert"),
        P(None, "expert"),
        P(None, "section", "expert", None),
        P("section", None),
        P("section", None),
        P("section", None),
        P("section", None),
        P("section", None, None),
        P("section", "expert", None, None, "dp"),
        P("section", "expert", "dp", None),
    )
    out_specs = P(None, "section", "expert", None)
    return jax.shard_map(body, mesh=mesh, in_specs=in_specs, out_specs=out_specs, check_vma=False)
```

```python
import functools

import jax
import jax.numpy as jnp
from jax import lax
from jax.experimental import pallas as pl
from jax.experimental.pallas import tpu as pltpu
from jax.sharding import PartitionSpec as P

HEAD_DIM = 128
LANES = 128
EPS = 1e-06
F32 = jnp.float32
BF16 = jnp.bfloat16
MIB = 1024 * 1024


def params(mib):
    return pltpu.CompilerParams(vmem_limit_bytes=mib * MIB)


def cost():
    return pl.CostEstimate(flops=1, bytes_accessed=1, transcendentals=0)


def vmem():
    return pl.BlockSpec(memory_space=pltpu.VMEM)


def smem():
    return pl.BlockSpec(memory_space=pltpu.SMEM)


def to_next_block(array, sections):
    count = lax.axis_size("expert")
    pairs = [(s * count + i, s * count + i + 1) for s in sections for i in range(count - 1)]
    return lax.ppermute(array, ("section", "expert"), pairs)


def to_next_phase(array, step, swap):
    count, planes = lax.axis_size("expert"), lax.axis_size("dp")
    pairs = []
    for e in range(count - step):
        for d in range(planes):
            target = (count + e + step) * planes + (planes - 1 - d if swap else d)
            pairs.append((e * planes + d, target))
    return lax.ppermute(array, ("section", "expert", "dp"), pairs)


def to_other_plane(array, sections):
    pairs = [(2 * s + d, 2 * s + 1 - d) for s in sections for d in (0, 1)]
    return lax.ppermute(array, ("section", "dp"), pairs)


def across(array, distance, sections):
    if distance == 0:
        return array
    count = lax.axis_size("expert")
    pairs = [(s * count + e, s * count + (e ^ distance)) for s in sections for e in range(count)]
    return lax.ppermute(array, ("section", "expert"), pairs)


def eye(size):
    return lax.broadcasted_iota(jnp.int32, (size, size), 0) == lax.broadcasted_iota(
        jnp.int32, (size, size), 1
    )


def as_column(row, diagonal):
    return jnp.sum(jnp.where(diagonal, row, 0.0), axis=1, keepdims=True)


def as_row(column, diagonal):
    return jnp.sum(jnp.where(diagonal, column, 0.0), axis=0, keepdims=True)


def dot(a, b, contract=((1,), (0,))):
    return lax.dot_general(a, b, (contract, ((), ())), preferred_element_type=F32)


def attend_kernel(merged, width, expert_count, scalar_ref, own_ref, prior_ref, *refs):
    meta_ref, prior_meta_ref, *refs = refs
    ids, scale = meta_ref[0:1, :], meta_ref[1:2, :]
    prior_ids, prior_scale = prior_meta_ref[0:1, :], prior_meta_ref[1:2, :]
    if merged:
        sent_ref, sent_prior_ref, ids_ref, prior_ids_ref, *refs = refs
        squares_ref, squares_other_ref, *refs = refs
        prior_squares_ref, prior_squares_other_ref, *refs = refs
        first = scalar_ref[1] == 0
        ids = jnp.where(first, ids, ids_ref[...])
        prior_ids = jnp.where(first, prior_ids, prior_ids_ref[...])
        passed = lax.rsqrt((squares_ref[...] + squares_other_ref[...]) / width + EPS)
        prior_passed = lax.rsqrt(
            (prior_squares_ref[...] + prior_squares_other_ref[...]) / width + EPS
        )
        scale = jnp.where(first, scale, passed)
        prior_scale = jnp.where(first, prior_scale, prior_passed)
    gain_ref, query_ref, key_ref, ffn_ref, router_ref, place_ref = refs[:6]
    residual_ref, stats_ref, *block_refs = refs[6:]
    rows, features = own_ref.shape
    diagonal = eye(rows)
    own_scale, prior_scale = as_column(scale, diagonal), as_column(prior_scale, diagonal)
    own_ids = as_column(ids, diagonal)
    causal = lax.broadcasted_iota(jnp.int32, (rows, rows), 1) <= lax.broadcasted_iota(
        jnp.int32, (rows, rows), 0
    )
    bias_own = jnp.where((own_ids == ids) & causal, 0.0, -1e30)
    bias_prior = jnp.where(own_ids == prior_ids, 0.0, -1e30)
    factor = HEAD_DIM ** (-0.5)
    squares = jnp.zeros((rows, HEAD_DIM), F32)
    scaled, sent_rows = [], []
    all_heads = features // HEAD_DIM
    batch = min(8, all_heads)
    for base in range(0, all_heads, batch):
        heads = [slice(h * HEAD_DIM, (h + 1) * HEAD_DIM) for h in range(base, base + batch)]
        owns, normeds, prior_normeds, scores = [], [], [], []
        for at in heads:
            gain = gain_ref[:, at].astype(F32)
            query_gain, key_gain = query_ref[:, at].astype(F32), key_ref[:, at].astype(F32)
            own, prior = own_ref[:, at], prior_ref[:, at]
            if merged:
                own = jnp.where(first, own, sent_ref[:, at])
                prior = jnp.where(first, prior, sent_prior_ref[:, at])
            own = own.astype(F32)
            normed = (own * own_scale * gain).astype(BF16)
            prior_normed = (prior.astype(F32) * prior_scale * gain).astype(BF16)
            queries = (normed.astype(F32) * query_gain).astype(BF16)
            keys = (normed.astype(F32) * key_gain).astype(BF16)
            prior_keys = (prior_normed.astype(F32) * key_gain).astype(BF16)
            owns.append(own)
            normeds.append(normed)
            prior_normeds.append(prior_normed)
            scores.append(
                (dot(queries, keys, ((1,), (1,))), dot(queries, prior_keys, ((1,), (1,))))
            )
        weights = []
        for score, prior_score in scores:
            score = score * factor + bias_own
            prior_score = prior_score * factor + bias_prior
            top = jnp.max(jnp.maximum(score, prior_score), axis=1, keepdims=True)
            raised, prior_raised = jnp.exp(score - top), jnp.exp(prior_score - top)
            inverse = 1.0 / jnp.sum(raised + prior_raised, axis=1, keepdims=True)
            weights.append(
                ((raised * inverse).astype(BF16), (prior_raised * inverse).astype(BF16))
            )
        for index, at in enumerate(heads):
            weight, prior_weight = weights[index]
            mixed = dot(weight, normeds[index]) + dot(prior_weight, prior_normeds[index])
            residual = owns[index] + mixed.astype(BF16).astype(F32)
            residual_ref[:, at] = residual
            squares = squares + residual * residual
            scaled.append((residual * ffn_ref[:, at].astype(F32)).astype(BF16))
            sent_rows.append(residual.astype(BF16))
    sent = dot(place_ref[...], jnp.concatenate(sent_rows, axis=1)).astype(BF16)
    start = 0
    for block_ref in block_refs:
        block_ref[...] = sent[start : start + block_ref.shape[0]]
        start += block_ref.shape[0]
    squares = jnp.sum(squares, axis=1, keepdims=True)
    logits = dot(jnp.concatenate(scaled, axis=1), router_ref[...], ((1,), (1,)))
    lane = lax.broadcasted_iota(jnp.int32, (rows, LANES), 1)
    stats_ref[...] = jnp.where(lane == expert_count, squares, logits)


def attend(merged, width, expert_count, plane, operands, gains, router, place):
    rows, features = operands[0].shape
    capacity = place.shape[0] // expert_count
    whole = lambda shape: pl.BlockSpec(shape, lambda step, plane_ref: (0, 0))
    side = lambda step, plane_ref: (0, plane_ref[0])
    in_specs = [whole(array.shape) for array in operands]
    in_specs += [pl.BlockSpec((1, features), side)] * len(gains)
    in_specs += [pl.BlockSpec((LANES, features), side), whole(place.shape)]
    shapes = [((rows, features), F32), ((rows, LANES), F32)]
    shapes += [((capacity, features), BF16)] * expert_count
    residual, stats, *blocks = pl.pallas_call(
        functools.partial(attend_kernel, merged, width, expert_count),
        out_shape=[jax.ShapeDtypeStruct(*shape) for shape in shapes],
        grid_spec=pltpu.PrefetchScalarGridSpec(
            num_scalar_prefetch=1,
            grid=(1,),
            in_specs=in_specs,
            out_specs=[whole(shape) for shape, _ in shapes],
        ),
        compiler_params=params(16),
        cost_estimate=cost(),
        name="attend",
    )(plane, *operands, *gains, router, place)
    return residual, stats, blocks


def expert_kernel(blocks, width, scalar_ref, *refs):
    own_refs, far_refs, refs = refs[:blocks], refs[blocks : 2 * blocks], refs[2 * blocks :]
    up_ref, down_ref, gain_ref, *refs = refs
    away_refs, kept_refs = refs[:blocks], refs[blocks : 2 * blocks]
    rows_ref, sum_ref, inner_ref, up_held, down_held, up_sems, down_sems = refs[2 * blocks :]
    slots, half = rows_ref.shape[1:]
    hidden = down_ref.shape[0]
    plane = scalar_ref[0]
    sides = (plane * half, (1 - plane) * half)
    depth = up_held.shape[1]
    parts = half // depth
    down_depth = down_held.shape[1]

    copies = []
    for index in range(2 * parts):
        first = pl.multiple_of(sides[index // parts] + index % parts * depth, depth)
        copies.append(
            pltpu.make_async_copy(
                up_ref.at[pl.ds(first, depth)], up_held.at[index], up_sems.at[index]
            )
        )
    down_copies = [
        pltpu.make_async_copy(
            down_ref.at[pl.ds(index * down_depth, down_depth)],
            down_held.at[index],
            down_sems.at[index],
        )
        for index in range(hidden // down_depth)
    ]
    for copy in copies + down_copies:
        copy.start()

    scales = []
    start = 0
    for own_ref, far_ref in zip(own_refs, far_refs):
        at = slice(start, start + own_ref.shape[0])
        start += own_ref.shape[0]
        squares = 0.0
        for which, source_ref in enumerate((own_ref, far_ref)):
            lanes = pl.ds(pl.multiple_of(sides[which], half), half)
            rows = source_ref[...].astype(F32)
            squares = squares + jnp.sum(rows * rows, axis=1, keepdims=True)
            rows_ref[which, at, :] = (rows * gain_ref[:, lanes].astype(F32)).astype(BF16)
        scales.append(lax.rsqrt(squares / width + EPS))
    scale = jnp.concatenate(scales, axis=0)

    columns = min(512, hidden)
    for index, copy in enumerate(copies):
        copy.wait()
        lanes = slice(index % parts * depth, (index % parts + 1) * depth)

        @pl.loop(0, 2 * hidden // columns)
        def _(step, index=index, lanes=lanes):
            at = pl.ds(pl.multiple_of(step * columns, columns), columns)
            made = dot(rows_ref[index // parts, :, lanes], up_held[index, :, at])
            sum_ref[:, at] = made if index == 0 else sum_ref[:, at] + made

    gate = sum_ref[:, :hidden] * scale
    value = sum_ref[:, hidden:] * scale
    inner_ref[...] = (gate / (1.0 + jnp.exp(-gate)) * value).astype(BF16)
    for copy in down_copies:
        copy.wait()
    columns = min(512, half)
    for target_refs, side in ((away_refs, sides[1]), (kept_refs, sides[0])):

        @pl.loop(0, half // columns)
        def _(step, target_refs=target_refs, side=side):
            first = pl.multiple_of(step * columns, columns)
            at = pl.ds(pl.multiple_of(side + first, columns), columns)
            made = 0.0
            for index in range(hidden // down_depth):
                inner = inner_ref[:, index * down_depth : (index + 1) * down_depth]
                made = made + dot(inner, down_held[index, :, at])
            start = 0
            for ref in target_refs:
                piece = made[start : start + ref.shape[0]]
                ref[:, pl.ds(first, columns)] = piece.astype(ref.dtype)
                start += ref.shape[0]


def expert_rows(scalars, own, far, up, down, gain):
    blocks = len(own)
    slots = sum(array.shape[0] for array in own)
    half = own[0].shape[1]
    hidden, width = down.shape
    depth, down_depth = min(1024, half), min(256, hidden)
    anywhere = pl.BlockSpec(memory_space=pl.ANY)
    outs = pl.pallas_call(
        functools.partial(expert_kernel, blocks, width),
        out_shape=[jax.ShapeDtypeStruct(array.shape, BF16) for array in (*own, *own)],
        in_specs=[smem()] + [vmem()] * (2 * blocks) + [anywhere, anywhere, vmem()],
        out_specs=[vmem()] * (2 * blocks),
        scratch_shapes=[
            pltpu.VMEM((2, slots, half), BF16),
            pltpu.VMEM((slots, 2 * hidden), F32),
            pltpu.VMEM((slots, hidden), BF16),
            pltpu.VMEM((width // depth, depth, 2 * hidden), BF16),
            pltpu.VMEM((hidden // down_depth, down_depth, width), BF16),
            pltpu.SemaphoreType.DMA((width // depth,)),
            pltpu.SemaphoreType.DMA((hidden // down_depth,)),
        ],
        compiler_params=params(32),
        cost_estimate=cost(),
        name="expert_rows",
    )(scalars, *own, *far, up, down, gain)
    return list(outs[:blocks]), list(outs[blocks:])


def combine_kernel(expert_count, width, *refs):
    *rows_refs, residual_ref, stats_ref, stats_other_ref, place_ref, made_ref, squares_ref = refs
    tokens, slots = place_ref.shape
    capacity = slots // expert_count
    stats = stats_ref[...] + stats_other_ref[...]
    lane = lax.broadcasted_iota(jnp.int32, (tokens, LANES), 1)
    total = jnp.sum(jnp.where(lane == expert_count, stats, 0.0), axis=1, keepdims=True)
    logits = stats * lax.rsqrt(total / width + EPS)
    expert = lax.broadcasted_iota(jnp.int32, (LANES, slots), 0)
    slot = lax.broadcasted_iota(jnp.int32, (LANES, slots), 1)
    spread = jnp.where(
        (slot >= expert * capacity) & (slot < (expert + 1) * capacity), 1.0, 0.0
    ).astype(BF16)
    place = place_ref[...]
    member = dot(place, spread, ((1,), (1,))) > 0.5
    logits = jnp.where(member, logits, -1e30)
    raised = jnp.exp(logits - jnp.max(logits, axis=1, keepdims=True))
    gates = raised / jnp.sum(raised, axis=1, keepdims=True)
    high = gates.astype(BF16)
    low = (gates - high.astype(F32)).astype(BF16)
    place = place.astype(F32)
    rows = jnp.concatenate([ref[...] for ref in rows_refs], axis=0)
    made = dot((dot(high, spread) * place).astype(BF16), rows)
    made = made + dot((dot(low, spread) * place).astype(BF16), rows)
    made = (residual_ref[...] + made).astype(BF16)
    made_ref[...] = made
    wide = made.astype(F32)
    squares_ref[...] = as_row(jnp.sum(wide * wide, axis=1, keepdims=True), eye(tokens))


def combine(expert_count, width, returned, residual, stats, stats_other, place):
    tokens, features = residual.shape
    return pl.pallas_call(
        functools.partial(combine_kernel, expert_count, width),
        out_shape=(
            jax.ShapeDtypeStruct((tokens, features), BF16),
            jax.ShapeDtypeStruct((1, tokens), F32),
        ),
        in_specs=[vmem()] * (len(returned) + 4),
        out_specs=(vmem(), vmem()),
        compiler_params=params(16),
        cost_estimate=cost(),
        name="combine",
    )(*returned, residual, stats, stats_other, place)


def body(
    hidden_held,
    fresh_rows,
    doc_held,
    doc_fresh,
    routes,
    attn_gain,
    query_gain,
    key_gain,
    ffn_gain,
    router,
    weight_in,
    weight_out,
):
    ticks = routes.shape[0]
    assert ticks == 2 and lax.axis_size("section") == 2 and lax.axis_size("dp") == 2
    tokens, width = hidden_held.shape[1:]
    top_count = routes.shape[3]
    count = router.shape[2]
    assert count == lax.axis_size("expert")
    capacity = min(tokens, 3 * tokens * top_count // (2 * count))
    capacity = -(-capacity // 16) * 16
    section = lax.axis_index("section").astype(jnp.int32)
    plane = lax.axis_index("dp").astype(jnp.int32)
    here = lax.axis_index("expert").astype(jnp.int32)
    half = width // 2
    scalars = jnp.stack([plane, section])
    both = (0, 1)

    def half_of(rows):
        return lax.dynamic_slice_in_dim(rows, plane * half, half, 1)

    def meta_of(rows, ids):
        wide = rows.astype(F32)
        scale = lax.rsqrt(jnp.mean(wide * wide, axis=1) + EPS)
        return jnp.stack([(ids + 1).astype(F32), scale])

    held = half_of(hidden_held[0])
    held_prior = to_next_block(held, both)
    held_meta = meta_of(hidden_held[0], doc_held[0])
    held_prior_meta = to_next_block(held_meta, both)

    labels = jnp.arange(count, dtype=jnp.int32)
    gains = [attn_gain, query_gain, key_gain, ffn_gain]
    wanted = (jnp.arange(LANES, dtype=jnp.int32)[:, None] == (labels ^ here)[None, :]).astype(BF16)
    router_rows = jnp.dot(wanted, router[0].T, preferred_element_type=F32).astype(BF16)
    up_weight = weight_in[0, 0].reshape(width, -1)
    down_weight = weight_out[0, 0]

    chosen = routes[:, 0] ^ here
    member = jnp.sum((chosen[..., None] == labels).astype(F32), axis=2)
    before = jnp.tril(jnp.ones((tokens, tokens), F32), -1)
    ranking = jnp.einsum("ij,tje->tie", before, member).astype(jnp.int32)
    ranking = jnp.where(member > 0, ranking, -1)
    slot = jnp.arange(capacity, dtype=jnp.int32)
    combine_place = (ranking[:, :, :, None] == slot).astype(BF16)
    combine_place = combine_place.reshape(ticks, tokens, count * capacity)
    send_place = (ranking.transpose(0, 2, 1)[:, :, None, :] == slot[:, None]).astype(BF16)
    send_place = send_place.reshape(ticks, count * capacity, tokens)

    near = range(count // 2)
    far, farther = range(count // 2, 3 * count // 4), range(3 * count // 4, count)

    def exchange(blocks):
        got = list(blocks)
        for k in [*far, *near]:
            got[k] = across(blocks[k], k, both)
        for k, sooner in zip(farther, far):
            block, got[sooner] = lax.optimization_barrier((blocks[k], got[sooner]))
            got[k] = across(block, k, both)
        return got

    def experts(own, hurry):
        other = [to_other_plane(block, both) for block in own]
        if hurry:
            other[0], rest = lax.optimization_barrier((other[0], [own[k] for k in farther]))
            for k, block in zip(farther, rest):
                own[k] = block
        away, kept = [], []
        for group in ([*near, *far], farther):
            mine, theirs = [own[k] for k in group], [other[k] for k in group]
            if kept:
                theirs[0], kept[0] = lax.optimization_barrier((theirs[0], kept[0]))
            made = expert_rows(scalars, mine, theirs, up_weight, down_weight, ffn_gain)
            away += made[0]
            kept += made[1]
        received = [None] * count
        for k in [*far, *farther]:
            received[k] = to_other_plane(away[k], both)
        for k in near:
            later = far[k % len(far)]
            block, received[later] = lax.optimization_barrier((away[k], received[later]))
            received[k] = to_other_plane(block, both)
        return [k + r for k, r in zip(kept, received)]

    def whole_rows(made, other):
        low, high = jnp.where(plane == 0, made, other), jnp.where(plane == 0, other, made)
        return jnp.concatenate([low, high], axis=1)

    ids = held_meta[0:1]
    sent_ids = [to_next_phase(ids, step, False) for step in (0, 1)]
    held_meta, up_weight, *sent_ids = lax.optimization_barrier((held_meta, up_weight, *sent_ids))
    residual, stats, rows = attend(
        False, width, count, scalars, [held, held_prior, held_meta, held_prior_meta],
        gains, router_rows, send_place[0],
    )
    stats_other = to_other_plane(stats, both)
    rows = exchange(rows)
    entry = far[-1]
    rows[entry], fresh_rows, doc_fresh = lax.optimization_barrier(
        (rows[entry], fresh_rows, doc_fresh)
    )
    fresh = half_of(fresh_rows[0])
    fresh_prior = to_next_block(fresh, (0,))
    fresh_meta = meta_of(fresh_rows[0], doc_fresh[0])
    fresh_prior_meta = to_next_block(fresh_meta, (0,))
    rows[1], fresh_prior, fresh_prior_meta = lax.optimization_barrier(
        (rows[1], fresh_prior, fresh_prior_meta)
    )
    returned = exchange(experts(rows, False))
    made, squares = combine(
        count, width, returned, residual, stats, stats_other, combine_place[0]
    )

    sent_prior, sent = to_next_phase(made, 1, False), to_next_phase(made, 0, False)
    scales = [to_next_phase(squares, step, swap) for step in (0, 1) for swap in (False, True)]
    other = to_other_plane(made, both)
    sent, other = lax.optimization_barrier((sent, other))
    results = [whole_rows(made, other)]
    residual, stats, rows = attend(
        True, width, count, scalars,
        [fresh, fresh_prior, fresh_meta, fresh_prior_meta, sent, sent_prior, *sent_ids, *scales],
        gains, router_rows, send_place[1],
    )
    stats_other = to_other_plane(stats, both)
    returned = exchange(experts(exchange(rows), True))
    made, squares = combine(
        count, width, returned, residual, stats, stats_other, combine_place[1]
    )
    results.append(whole_rows(made, to_other_plane(made, both)))
    return jnp.stack(results)[:, None]


def solution(mesh):
    in_specs = (
        P("section", "expert", None),
        P(None, "expert", None),
        P("section", "expert"),
        P(None, "expert"),
        P(None, "section", "expert", None),
        P("section", None),
        P("section", None),
        P("section", None),
        P("section", None),
        P("section", None, None),
        P("section", "expert", None, None, "dp"),
        P("section", "expert", "dp", None),
    )
    out_specs = P(None, "section", "expert", None)
    return jax.shard_map(body, mesh=mesh, in_specs=in_specs, out_specs=out_specs, check_vma=False)
```
